32 devices in a mesh: inner: 4 (over x, core), outer: 2 (over y), tile: 4 (over z).
Axes of the slice: x: 2, y: 2, z: 4, core: 2. Of those that a mesh axis runs over, the one named last changes fastest.
Arguments:
- density: bfloat16 [128, 256, 2048], P(('inner', 'outer'), None, 'tile'), parts along dimension 2, may hold values from 0.049804688 to 1
- extinction: float32 [128], P(('inner', 'outer')), may hold values from 0.0002 to 0.01
- occupancy: int32 [8, 16, 128], P(('inner', 'outer'), None, 'tile'), parts along dimension 2, may hold values 0 or 1
- colour_slope: float32 [3], replicated, may hold values from -6 to 6
- slab_rank: int32 [8], replicated, may hold values from 0 to 7, as said below
Outputs:
- image: float32 [4, 256, 2048], P(None, 'inner', ('tile', 'outer')), parts along dimension 2
The draws below stay inside these ranges and needn't reach their ends.
There are 4 independent parts, one for each index of `tile`. The reference program is written for one: setup_inputs(seed, part) draws one part's arguments, and reference() takes and returns one part's arrays. A program takes and returns all parts, laid end to end along the dimension named above; an argument that names none is the same for every part. Nothing has to cross between parts.
Inputs may be any that keep to these rules, and one draw needn't show every extreme that they name: slab_rank is a permutation of 0 to 7; the slabs whose index leaves the same remainder modulo 2 hold 4 consecutive ranks.
All inputs are finite; a program needn't handle non-finite values. No bound on the sum of `occupancy` on one device may be relied on, other than what follows from the above.
Results may differ from the reference program's by a relative error of at most 0.0003.
Values sent between devices are 32-bit elements; how exact they have to be, the bound alone decides.
A program may use at most 64 MiB of HBM per device.

```python
import math
import jax
import jax.numpy as jnp
from jax import lax

H = 256
W = 512
SL_DEV = 16
BLOCK = 16
INNER_SLABS = 4
OUTER_GROUPS = 2
SLABS = 8
SLICES = 128


def draw_slab_rank(key, part):
    key = jax.random.fold_in(key, 7)
    first_key, second_key = jax.random.split(key)
    group_order = jax.random.permutation(first_key, OUTER_GROUPS)
    row_keys = jax.random.split(second_key, OUTER_GROUPS)
    inner_order = jax.vmap(lambda row_key: jax.random.permutation(row_key, INNER_SLABS))(row_keys)
    ranking = group_order[:, None] * INNER_SLABS + inner_order
    return ranking.T.reshape(-1).astype(jnp.int32)


def with_ends(values, stream_key, smallest, high):
    longest = values.shape.index(max(values.shape))
    spots = []
    for shift in (0, 1):
        where = [jax.random.randint(jax.random.fold_in(stream_key, axis), (), 0, length) for axis, length in enumerate(values.shape)]
        where[longest] = (where[longest] + shift) % values.shape[longest]
        spots.append(tuple(where))
    return values.at[spots[0]].set(smallest).at[spots[1]].set(high)


def block_levels(rng, dims, shards, smallest, high):
    level = 1.0
    for position, shards_of in shards:
        draws = jax.random.uniform(jax.random.fold_in(jax.random.fold_in(rng, 6), position), (shards_of,), jnp.float32, smallest / len(shards), high / len(shards))
        level = level * jnp.repeat(jnp.exp(draws), dims[position] // shards_of).reshape((-1,) + (1,) * (len(dims) - 1 - position))
    return level


def setup_inputs(seed: int = 0, part: int = 0) -> dict:
    key_list = jax.random.split(jax.random.key(seed), 6)
    part_splits = jax.random.split(jax.random.fold_in(key_list[5], part), 6)
    return {
        "density": jnp.clip(jnp.exp(math.log(1.0) - 2.9996462 * jax.random.uniform(part_splits[0], (SLICES, H, W), jnp.float32) ** block_levels(part_splits[0], (SLICES, H, W), ((0, 8),), -0.2, 0.2)), 0.049804688, 1.0).astype(jnp.bfloat16),
        "extinction": jnp.clip(jnp.exp(math.log(0.01) - 3.912023 * jax.random.uniform(key_list[1], (SLICES,), jnp.float32) ** block_levels(key_list[1], (SLICES,), ((0, 8),), -0.2, 0.2)), 0.0002, 0.01),
        "occupancy": with_ends((jax.random.randint(part_splits[2], (SLABS, H // BLOCK, W // BLOCK), 0, 4) < 3).astype(jnp.int32), jax.random.fold_in(part_splits[2], 1), 0, 1),
        "colour_slope": jnp.clip(jax.random.uniform(key_list[3], (3,), jnp.float32, -6.0, 6.0), -6.0, 6.0),
        "slab_rank": draw_slab_rank(jax.random.fold_in(key_list[5], 71), part),
    }


def march(density, extinction, occupancy, colour_slope):
    blocks = occupancy[0].astype(jnp.float32)
    filled = jnp.repeat(jnp.repeat(blocks, density.shape[1] // blocks.shape[0], axis=0), density.shape[2] // blocks.shape[1], axis=1)

    def advance(carry, inputs):
        colour_sum, through = carry
        layer, absorb = inputs
        sample = layer.astype(jnp.float32) * filled
        opacity = 1.0 - jnp.exp(-absorb * sample)
        colour = jax.nn.sigmoid(colour_slope[:, None, None] * (sample - 0.3))
        colour_sum = colour_sum + (through * opacity)[None] * colour
        through = through * (1.0 - opacity)
        return (colour_sum, through), None

    start = (jnp.zeros((3,) + density.shape[1:], jnp.float32), jnp.ones(density.shape[1:], jnp.float32))
    (colour_sum, through), unused = lax.scan(advance, start, (density, extinction))
    return jnp.concatenate([colour_sum, through[None]], axis=0)


def reference(density, extinction, occupancy, colour_slope, slab_rank):
    order = jnp.argsort(slab_rank).astype(jnp.int32)

    def visit(carry, slab):
        colour_sum, through = carry
        layer = lax.dynamic_slice_in_dim(density, slab * SL_DEV, SL_DEV, 0)
        absorb = lax.dynamic_slice_in_dim(extinction, slab * SL_DEV, SL_DEV, 0)
        blocks = lax.dynamic_slice_in_dim(occupancy, slab, 1, 0)
        piece = march(layer, absorb, blocks, colour_slope)
        return (colour_sum + through[None] * piece[:3], through * piece[3]), None

    start = (jnp.zeros((3, H, W), jnp.float32), jnp.ones((H, W), jnp.float32))
    (colour_sum, through), unused = lax.scan(visit, start, order)
    return jnp.concatenate([colour_sum, (1.0 - through)[None]], axis=0)
```

```python
import functools

import jax
import jax.numpy as jnp
from jax import lax
from jax.experimental import pallas as pl
from jax.experimental.pallas import tpu as pltpu
from jax.sharding import PartitionSpec as P


def march(density, extinction, occupancy, colour_slope):
    blocks = occupancy[0].astype(jnp.float32)
    filled = jnp.repeat(
        jnp.repeat(blocks, density.shape[1] // blocks.shape[0], axis=0),
        density.shape[2] // blocks.shape[1],
        axis=1,
    )

    def advance(carry, inputs):
        colour_sum, through = carry
        layer, absorb = inputs
        sample = layer.astype(jnp.float32) * filled
        opacity = 1.0 - jnp.exp(-absorb * sample)
        colour = jax.nn.sigmoid(colour_slope[:, None, None] * (sample - 0.3))
        colour_sum = colour_sum + (through * opacity)[None] * colour
        through = through * (1.0 - opacity)
        return ((colour_sum, through), None)

    start = (
        jnp.zeros((3,) + density.shape[1:], jnp.float32),
        jnp.ones(density.shape[1:], jnp.float32),
    )
    (colour_sum, through), unused = lax.scan(advance, start, (density, extinction))
    return jnp.concatenate([colour_sum, through[None]], axis=0)


def composite(pieces, ranks):
    count = pieces.shape[0]
    select = (ranks[None, :] == jnp.arange(count, dtype=jnp.int32)[:, None]).astype(jnp.float32)
    ordered = jnp.einsum("kj,jchw->kchw", select, pieces, precision=lax.Precision.HIGHEST)
    running = jnp.cumprod(ordered[:, 3], axis=0)
    front = jnp.concatenate([jnp.ones_like(running[:1]), running[:-1]], axis=0)
    colour = jnp.sum(ordered[:, :3] * front[:, None], axis=0)
    return jnp.concatenate([colour, running[-1:]], axis=0)


def shards(density, extinction, occupancy, colour_slope, slab_rank):
    pieces = march(density, extinction, occupancy, colour_slope)
    inner_count = lax.axis_size("inner")
    outer_count = lax.axis_size("outer")
    rank_grid = slab_rank.reshape(inner_count, outer_count)
    mine = lax.dynamic_index_in_dim(rank_grid, lax.axis_index("outer"), 1, keepdims=False)
    arrived = lax.all_to_all(pieces[None], "inner", split_axis=2, concat_axis=0, tiled=True)
    banded = composite(arrived, mine - jnp.min(mine))
    group_rank = jnp.min(rank_grid, axis=0) // inner_count
    arrived_groups = lax.all_to_all(banded[None], "outer", split_axis=3, concat_axis=0, tiled=True)
    total = composite(arrived_groups, group_rank)
    return jnp.concatenate([total[:3], 1.0 - total[3:]], axis=0)


ROWS = 16
COLS = 256
MESH = pl.DeviceIdType.MESH


def fused_kernel(
    inner_count, outer_count,
    density, extinction, occupancy, slope, rank, out,
    field, fill, pieces, arrived, banded, groups,
    load_sem, send_sem, recv_sem, outer_send_sem, outer_recv_sem,
):
    slices, height, width = field.shape
    band = height // inner_count
    chunks = band // ROWS
    part = width // outer_count
    me = lax.axis_index("inner")
    group = lax.axis_index("outer")

    pairs = inner_count // 2
    chip, core = me // 2, me % 2
    partners = []
    for step in range(1, pairs):
        other = lax.rem(chip + step, pairs)
        partners += [other * 2 + core, other * 2 + (1 - core)]
    partners.append(chip * 2 + (1 - core))
    outer_partners = [lax.rem(group + step, outer_count) for step in range(1, outer_count)]

    def load(owner):
        rows = pl.ds(pl.multiple_of(owner * band, ROWS), band)
        return pltpu.make_async_copy(
            density.at[:, rows, :], field.at[:, rows, :], load_sem.at[owner]
        )

    for owner in partners + [me]:
        load(owner).start()

    barrier = pltpu.get_barrier_semaphore()
    for partner in partners:
        pl.semaphore_signal(barrier, inc=1, device_id={"inner": partner}, device_id_type=MESH)
    for partner in outer_partners:
        pl.semaphore_signal(barrier, inc=1, device_id={"outer": partner}, device_id_type=MESH)

    block_rows, block_columns = occupancy.shape[1:]
    spread = (
        lax.broadcasted_iota(jnp.int32, (block_columns, width), 1) // (width // block_columns)
        == lax.broadcasted_iota(jnp.int32, (block_columns, width), 0)
    ).astype(jnp.float32)
    fill[...] = jnp.dot(
        occupancy[0].astype(jnp.float32), spread, preferred_element_type=jnp.float32
    )

    half = [slope[k] * 0.5 for k in range(3)]
    block_height = height // block_rows

    def march(owner, chunk):
        start = pl.multiple_of(owner * band + chunk * ROWS, ROWS)
        to = pl.ds(pl.multiple_of(chunk * ROWS, ROWS), ROWS)
        for column in range(0, width, COLS):
            columns = slice(column, column + COLS)
            through = jnp.ones((ROWS, COLS), jnp.float32)
            sums = [jnp.zeros((ROWS, COLS), jnp.float32) for k in range(3)]
            for t in range(slices):
                sample = field[t, pl.ds(start, ROWS), columns].astype(jnp.float32)
                after = through * jnp.exp2(sample * (extinction[t] * -1.4426950408889634))
                weight = through - after
                through = after
                shifted = sample - 0.3
                sums = [sums[k] + weight * jnp.tanh(half[k] * shifted) for k in range(3)]
            full = fill[pl.ds(start // block_height, 1), columns] > 0.5
            for k in range(3):
                pieces[owner, k, to, columns] = jnp.where(
                    full, 0.5 * ((1.0 - through) + sums[k]), 0.0
                )
            pieces[owner, 3, to, columns] = jnp.where(full, through, 1.0)

    def rows_of(chunk):
        return pl.ds(pl.multiple_of(chunk * ROWS, ROWS), ROWS)

    def send(partner, chunk):
        return pltpu.make_async_remote_copy(
            src_ref=pieces.at[partner, :, rows_of(chunk), :],
            dst_ref=arrived.at[me, :, rows_of(chunk), :],
            send_sem=send_sem.at[partner, chunk],
            recv_sem=recv_sem.at[me, chunk],
            device_id={"inner": partner},
            device_id_type=MESH,
        )

    def receive(partner, chunk):
        return pltpu.make_async_remote_copy(
            src_ref=pieces.at[partner, :, rows_of(chunk), :],
            dst_ref=arrived.at[partner, :, rows_of(chunk), :],
            send_sem=send_sem.at[partner, chunk],
            recv_sem=recv_sem.at[partner, chunk],
            device_id={"inner": partner},
            device_id_type=MESH,
        )

    def outer_copy(partner, slot, chunk):
        return pltpu.make_async_remote_copy(
            src_ref=banded.at[:, rows_of(chunk), pl.ds(pl.multiple_of(partner * part, 128), part)],
            dst_ref=groups.at[slot, :, rows_of(chunk), :],
            send_sem=outer_send_sem.at[partner, chunk],
            recv_sem=outer_recv_sem.at[slot, chunk],
            device_id={"outer": partner},
            device_id_type=MESH,
        )

    far = partners[:-1]
    near = partners[-1]
    for index, owner in enumerate(far):
        load(owner).wait()
        if index == 0:
            pl.semaphore_wait(barrier, len(partners) + len(outer_partners))

    @pl.loop(0, chunks)
    def _(chunk):
        for owner in far:
            march(owner, chunk)
            send(owner, chunk).start()

    load(near).wait()
    load(me).wait()

    @pl.loop(0, chunks)
    def _(chunk):
        march(near, chunk)
        send(near, chunk).start()
        march(me, chunk)

    def fronts(values, ranks):
        found = []
        for k in range(len(values)):
            front = None
            for j in range(len(values)):
                if j != k:
                    factor = jnp.where(ranks[j] < ranks[k], values[j], 1.0)
                    front = factor if front is None else front * factor
            found.append(front)
        return found

    def product(values):
        result = values[0]
        for value in values[1:]:
            result = result * value
        return result

    slabs = partners + [me]
    slab_ranks = [rank[slab * outer_count + group] for slab in slabs]

    @pl.loop(0, chunks)
    def _(chunk):
        for partner in partners:
            receive(partner, chunk).wait_recv()
        rows = rows_of(chunk)
        for column in range(0, width, 128):
            columns = slice(column, column + 128)

            def value(slab, k):
                source = pieces if slab is me else arrived
                return source[slab, k, rows, columns]

            clear = [value(slab, 3) for slab in slabs]
            weights = fronts(clear, slab_ranks)
            for k in range(3):
                banded[k, rows, columns] = sum(
                    weights[i] * value(slab, k) for i, slab in enumerate(slabs)
                )
            banded[3, rows, columns] = product(clear)
        for partner in outer_partners:
            outer_copy(partner, group, chunk).start()

    ordered = outer_partners + [group]
    group_ranks = [rank[g] for g in ordered]
    mine = pl.ds(pl.multiple_of(group * part, 128), part)

    @pl.loop(0, chunks)
    def _(chunk):
        for partner in outer_partners:
            outer_copy(group, partner, chunk).wait_recv()
        rows = rows_of(chunk)

        def value(g, k):
            if g is group:
                return banded[k, rows, mine]
            return groups[g, k, rows, :]

        clear = [value(g, 3) for g in ordered]
        weights = fronts(clear, group_ranks)
        for k in range(3):
            out[k, rows, :] = sum(weights[i] * value(g, k) for i, g in enumerate(ordered))
        out[3, rows, :] = 1.0 - product(clear)

    @pl.loop(0, chunks)
    def _(chunk):
        for partner in partners:
            send(partner, chunk).wait_send()
        for partner in outer_partners:
            outer_copy(partner, group, chunk).wait_send()


def fused(density, extinction, occupancy, colour_slope, slab_rank):
    inner_count = lax.axis_size("inner")
    outer_count = lax.axis_size("outer")
    slices, height, width = density.shape
    band, part = height // inner_count, width // outer_count
    chunks = band // ROWS
    vmem = pl.BlockSpec(memory_space=pltpu.VMEM)
    smem = pl.BlockSpec(memory_space=pltpu.SMEM)
    return pl.pallas_call(
        functools.partial(fused_kernel, inner_count, outer_count),
        out_shape=jax.ShapeDtypeStruct((4, band, part), jnp.float32),
        in_specs=[pl.BlockSpec(memory_space=pl.ANY), smem, vmem, smem, smem],
        out_specs=vmem,
        scratch_shapes=[
            pltpu.VMEM((slices, height, width), density.dtype),
            pltpu.VMEM((occupancy.shape[1], width), jnp.float32),
            pltpu.VMEM((inner_count, 4, band, width), jnp.float32),
            pltpu.VMEM((inner_count, 4, band, width), jnp.float32),
            pltpu.VMEM((4, band, width), jnp.float32),
            pltpu.VMEM((outer_count, 4, band, part), jnp.float32),
            pltpu.SemaphoreType.DMA((inner_count,)),
            pltpu.SemaphoreType.DMA((inner_count, chunks)),
            pltpu.SemaphoreType.DMA((inner_count, chunks)),
            pltpu.SemaphoreType.DMA((outer_count, chunks)),
            pltpu.SemaphoreType.DMA((outer_count, chunks)),
        ],
        compiler_params=pltpu.CompilerParams(
            collective_id=0, has_side_effects=True, vmem_limit_bytes=40 * 2**20
        ),
    )(density, extinction, occupancy, colour_slope, slab_rank)


def solution(mesh):
    placed = (
        P(("inner", "outer"), None, "tile"),
        P(("inner", "outer")),
        P(("inner", "outer"), None, "tile"),
        P(),
        P(),
    )

    def local(density, *rest):
        part = density.shape[2] // mesh.shape["outer"]
        band = density.shape[1] // mesh.shape["inner"]
        whole = part % 128 == 0 and band % ROWS == 0 and mesh.shape["inner"] % 2 == 0
        return (fused if whole else shards)(density, *rest)

    return jax.shard_map(
        local,
        mesh=mesh,
        in_specs=placed,
        out_specs=P(None, "inner", ("tile", "outer")),
        check_vma=False,
    )
```

```python
import functools

import jax
import jax.numpy as jnp
from jax import lax
from jax.experimental import pallas as pl
from jax.experimental.pallas import tpu as pltpu
from jax.sharding import PartitionSpec as P


def march(density, extinction, occupancy, colour_slope):
    blocks = occupancy[0].astype(jnp.float32)
    filled = jnp.repeat(
        jnp.repeat(blocks, density.shape[1] // blocks.shape[0], axis=0),
        density.shape[2] // blocks.shape[1],
        axis=1,
    )

    def advance(carry, inputs):
        colour_sum, through = carry
        layer, absorb = inputs
        sample = layer.astype(jnp.float32) * filled
        opacity = 1.0 - jnp.exp(-absorb * sample)
        colour = jax.nn.sigmoid(colour_slope[:, None, None] * (sample - 0.3))
        colour_sum = colour_sum + (through * opacity)[None] * colour
        through = through * (1.0 - opacity)
        return ((colour_sum, through), None)

    start = (
        jnp.zeros((3,) + density.shape[1:], jnp.float32),
        jnp.ones(density.shape[1:], jnp.float32),
    )
    (colour_sum, through), unused = lax.scan(advance, start, (density, extinction))
    return jnp.concatenate([colour_sum, through[None]], axis=0)


def composite(pieces, ranks):
    count = pieces.shape[0]
    select = (ranks[None, :] == jnp.arange(count, dtype=jnp.int32)[:, None]).astype(jnp.float32)
    ordered = jnp.einsum("kj,jchw->kchw", select, pieces, precision=lax.Precision.HIGHEST)
    running = jnp.cumprod(ordered[:, 3], axis=0)
    front = jnp.concatenate([jnp.ones_like(running[:1]), running[:-1]], axis=0)
    colour = jnp.sum(ordered[:, :3] * front[:, None], axis=0)
    return jnp.concatenate([colour, running[-1:]], axis=0)


def shards(density, extinction, occupancy, colour_slope, slab_rank):
    pieces = march(density, extinction, occupancy, colour_slope)
    inner_count = lax.axis_size("inner")
    outer_count = lax.axis_size("outer")
    rank_grid = slab_rank.reshape(inner_count, outer_count)
    mine = lax.dynamic_index_in_dim(rank_grid, lax.axis_index("outer"), 1, keepdims=False)
    arrived = lax.all_to_all(pieces[None], "inner", split_axis=2, concat_axis=0, tiled=True)
    banded = composite(arrived, mine - jnp.min(mine))
    group_rank = jnp.min(rank_grid, axis=0) // inner_count
    arrived_groups = lax.all_to_all(banded[None], "outer", split_axis=3, concat_axis=0, tiled=True)
    total = composite(arrived_groups, group_rank)
    return jnp.concatenate([total[:3], 1.0 - total[3:]], axis=0)


ROWS = 16
COLS = 256
MESH = pl.DeviceIdType.MESH


def fused_kernel(
    inner_count, outer_count,
    density, extinction_in, occupancy_in, slope_in, rank_in, out,
    extinction, occupancy, slope, rank,
    field, fill, pieces, arrived, banded, groups,
    small_sem, load_sem, send_sem, recv_sem, outer_send_sem, outer_recv_sem,
):
    slices, height, width = field.shape
    band = height // inner_count
    chunks = band // ROWS
    part = width // outer_count
    me = lax.axis_index("inner")
    group = lax.axis_index("outer")

    pairs = inner_count // 2
    chip, core = me // 2, me % 2
    partners = []
    for step in range(1, pairs):
        other = lax.rem(chip + step, pairs)
        partners += [other * 2 + core, other * 2 + (1 - core)]
    partners.append(chip * 2 + (1 - core))
    outer_partners = [lax.rem(group + step, outer_count) for step in range(1, outer_count)]

    def load(owner):
        rows = pl.ds(pl.multiple_of(owner * band, ROWS), band)
        return pltpu.make_async_copy(
            density.at[:, rows, :], field.at[:, rows, :], load_sem.at[owner]
        )

    small = [
        pltpu.make_async_copy(source, target, small_sem.at[index])
        for index, (source, target) in enumerate([
            (extinction_in, extinction), (occupancy_in, occupancy),
            (slope_in, slope), (rank_in, rank),
        ])
    ]
    for copy in small:
        copy.start()
    for owner in partners + [me]:
        load(owner).start()

    barrier = pltpu.get_barrier_semaphore()
    for partner in partners:
        pl.semaphore_signal(barrier, inc=1, device_id={"inner": partner}, device_id_type=MESH)
    for partner in outer_partners:
        pl.semaphore_signal(barrier, inc=1, device_id={"outer": partner}, device_id_type=MESH)

    for copy in small:
        copy.wait()

    block_rows, block_columns = occupancy.shape[1:]
    spread = (
        lax.broadcasted_iota(jnp.int32, (block_columns, width), 1) // (width // block_columns)
        == lax.broadcasted_iota(jnp.int32, (block_columns, width), 0)
    ).astype(jnp.float32)
    fill[...] = jnp.dot(
        occupancy[0].astype(jnp.float32), spread, preferred_element_type=jnp.float32
    )

    half = [slope[k] * 0.5 for k in range(3)]
    block_height = height // block_rows

    def march(owner, chunk):
        start = pl.multiple_of(owner * band + chunk * ROWS, ROWS)
        to = pl.ds(pl.multiple_of(chunk * ROWS, ROWS), ROWS)
        for column in range(0, width, COLS):
            columns = slice(column, column + COLS)
            through = jnp.ones((ROWS, COLS), jnp.float32)
            sums = [jnp.zeros((ROWS, COLS), jnp.float32) for k in range(3)]
            for t in range(slices):
                sample = field[t, pl.ds(start, ROWS), columns].astype(jnp.float32)
                after = through * jnp.exp2(sample * (extinction[t] * -1.4426950408889634))
                weight = through - after
                through = after
                shifted = sample - 0.3
                sums = [sums[k] + weight * jnp.tanh(half[k] * shifted) for k in range(3)]
            full = fill[pl.ds(start // block_height, 1), columns] > 0.5
            for k in range(3):
                pieces[owner, k, to, columns] = jnp.where(
                    full, 0.5 * ((1.0 - through) + sums[k]), 0.0
                )
            pieces[owner, 3, to, columns] = jnp.where(full, through, 1.0)

    def rows_of(chunk):
        return pl.ds(pl.multiple_of(chunk * ROWS, ROWS), ROWS)

    def send(partner, chunk):
        return pltpu.make_async_remote_copy(
            src_ref=pieces.at[partner, :, rows_of(chunk), :],
            dst_ref=arrived.at[me, :, rows_of(chunk), :],
            send_sem=send_sem.at[partner, chunk],
            recv_sem=recv_sem.at[me, chunk],
            device_id={"inner": partner},
            device_id_type=MESH,
        )

    def receive(partner, chunk):
        return pltpu.make_async_remote_copy(
            src_ref=pieces.at[partner, :, rows_of(chunk), :],
            dst_ref=arrived.at[partner, :, rows_of(chunk), :],
            send_sem=send_sem.at[partner, chunk],
            recv_sem=recv_sem.at[partner, chunk],
            device_id={"inner": partner},
            device_id_type=MESH,
        )

    def outer_copy(partner, slot, chunk):
        return pltpu.make_async_remote_copy(
            src_ref=banded.at[:, rows_of(chunk), pl.ds(pl.multiple_of(partner * part, 128), part)],
            dst_ref=groups.at[slot, :, rows_of(chunk), :],
            send_sem=outer_send_sem.at[partner, chunk],
            recv_sem=outer_recv_sem.at[slot, chunk],
            device_id={"outer": partner},
            device_id_type=MESH,
        )

    far = partners[:-1]
    near = partners[-1]
    for index, owner in enumerate(far):
        load(owner).wait()
        if index == 0:
            pl.semaphore_wait(barrier, len(partners) + len(outer_partners))

    @pl.loop(0, chunks)
    def _(chunk):
        for owner in far:
            march(owner, chunk)
            send(owner, chunk).start()

    load(near).wait()
    load(me).wait()

    @pl.loop(0, chunks)
    def _(chunk):
        march(near, chunk)
        send(near, chunk).start()
        march(me, chunk)

    def fronts(values, ranks):
        found = []
        for k in range(len(values)):
            front = None
            for j in range(len(values)):
                if j != k:
                    factor = jnp.where(ranks[j] < ranks[k], values[j], 1.0)
                    front = factor if front is None else front * factor
            found.append(front)
        return found

    def product(values):
        result = values[0]
        for value in values[1:]:
            result = result * value
        return result

    slabs = partners + [me]
    slab_ranks = [rank[slab * outer_count + group] for slab in slabs]

    @pl.loop(0, chunks)
    def _(chunk):
        for partner in partners:
            receive(partner, chunk).wait_recv()
        rows = rows_of(chunk)
        for column in range(0, width, 128):
            columns = slice(column, column + 128)

            def value(slab, k):
                source = pieces if slab is me else arrived
                return source[slab, k, rows, columns]

            clear = [value(slab, 3) for slab in slabs]
            weights = fronts(clear, slab_ranks)
            for k in range(3):
                banded[k, rows, columns] = sum(
                    weights[i] * value(slab, k) for i, slab in enumerate(slabs)
                )
            banded[3, rows, columns] = product(clear)
        for partner in outer_partners:
            outer_copy(partner, group, chunk).start()

    ordered = outer_partners + [group]
    group_ranks = [rank[g] for g in ordered]
    mine = pl.ds(pl.multiple_of(group * part, 128), part)

    @pl.loop(0, chunks)
    def _(chunk):
        for partner in outer_partners:
            outer_copy(group, partner, chunk).wait_recv()
        rows = rows_of(chunk)

        def value(g, k):
            if g is group:
                return banded[k, rows, mine]
            return groups[g, k, rows, :]

        clear = [value(g, 3) for g in ordered]
        weights = fronts(clear, group_ranks)
        for k in range(3):
            out[k, rows, :] = sum(weights[i] * value(g, k) for i, g in enumerate(ordered))
        out[3, rows, :] = 1.0 - product(clear)

    @pl.loop(0, chunks)
    def _(chunk):
        for partner in partners:
            send(partner, chunk).wait_send()
        for partner in outer_partners:
            outer_copy(partner, group, chunk).wait_send()


def fused(density, extinction, occupancy, colour_slope, slab_rank):
    inner_count = lax.axis_size("inner")
    outer_count = lax.axis_size("outer")
    slices, height, width = density.shape
    band, part = height // inner_count, width // outer_count
    chunks = band // ROWS
    vmem = pl.BlockSpec(memory_space=pltpu.VMEM)
    return pl.pallas_call(
        functools.partial(fused_kernel, inner_count, outer_count),
        out_shape=jax.ShapeDtypeStruct((4, band, part), jnp.float32),
        in_specs=[pl.BlockSpec(memory_space=pl.ANY)] * 5,
        out_specs=vmem,
        scratch_shapes=[
            pltpu.SMEM(extinction.shape, extinction.dtype),
            pltpu.VMEM(occupancy.shape, occupancy.dtype),
            pltpu.SMEM(colour_slope.shape, colour_slope.dtype),
            pltpu.SMEM(slab_rank.shape, slab_rank.dtype),
            pltpu.VMEM((slices, height, width), density.dtype),
            pltpu.VMEM((occupancy.shape[1], width), jnp.float32),
            pltpu.VMEM((inner_count, 4, band, width), jnp.float32),
            pltpu.VMEM((inner_count, 4, band, width), jnp.float32),
            pltpu.VMEM((4, band, width), jnp.float32),
            pltpu.VMEM((outer_count, 4, band, part), jnp.float32),
            pltpu.SemaphoreType.DMA((4,)),
            pltpu.SemaphoreType.DMA((inner_count,)),
            pltpu.SemaphoreType.DMA((inner_count, chunks)),
            pltpu.SemaphoreType.DMA((inner_count, chunks)),
            pltpu.SemaphoreType.DMA((outer_count, chunks)),
            pltpu.SemaphoreType.DMA((outer_count, chunks)),
        ],
        compiler_params=pltpu.CompilerParams(
            collective_id=0, has_side_effects=True, vmem_limit_bytes=60 * 2**20
        ),
    )(density, extinction, occupancy, colour_slope, slab_rank)


def solution(mesh):
    placed = (
        P(("inner", "outer"), None, "tile"),
        P(("inner", "outer")),
        P(("inner", "outer"), None, "tile"),
        P(),
        P(),
    )

    def local(density, *rest):
        part = density.shape[2] // mesh.shape["outer"]
        band = density.shape[1] // mesh.shape["inner"]
        whole = part % 128 == 0 and band % ROWS == 0 and mesh.shape["inner"] % 2 == 0
        return (fused if whole else shards)(density, *rest)

    return jax.shard_map(
        local,
        mesh=mesh,
        in_specs=placed,
        out_specs=P(None, "inner", ("tile", "outer")),
        check_vma=False,
    )
```

```python
import functools

import jax
import jax.numpy as jnp
from jax import lax
from jax.experimental import pallas as pl
from jax.experimental.pallas import tpu as pltpu
from jax.sharding import PartitionSpec as P


def march(density, extinction, occupancy, colour_slope):
    blocks = occupancy[0].astype(jnp.float32)
    filled = jnp.repeat(
        jnp.repeat(blocks, density.shape[1] // blocks.shape[0], axis=0),
        density.shape[2] // blocks.shape[1],
        axis=1,
    )

    def advance(carry, inputs):
        colour_sum, through = carry
        layer, absorb = inputs
        sample = layer.astype(jnp.float32) * filled
        opacity = 1.0 - jnp.exp(-absorb * sample)
        colour = jax.nn.sigmoid(colour_slope[:, None, None] * (sample - 0.3))
        colour_sum = colour_sum + (through * opacity)[None] * colour
        through = through * (1.0 - opacity)
        return ((colour_sum, through), None)

    start = (
        jnp.zeros((3,) + density.shape[1:], jnp.float32),
        jnp.ones(density.shape[1:], jnp.float32),
    )
    (colour_sum, through), unused = lax.scan(advance, start, (density, extinction))
    return jnp.concatenate([colour_sum, through[None]], axis=0)


def composite(pieces, ranks):
    count = pieces.shape[0]
    select = (ranks[None, :] == jnp.arange(count, dtype=jnp.int32)[:, None]).astype(jnp.float32)
    ordered = jnp.einsum("kj,jchw->kchw", select, pieces, precision=lax.Precision.HIGHEST)
    running = jnp.cumprod(ordered[:, 3], axis=0)
    front = jnp.concatenate([jnp.ones_like(running[:1]), running[:-1]], axis=0)
    colour = jnp.sum(ordered[:, :3] * front[:, None], axis=0)
    return jnp.concatenate([colour, running[-1:]], axis=0)


def shards(density, extinction, occupancy, colour_slope, slab_rank):
    pieces = march(density, extinction, occupancy, colour_slope)
    inner_count = lax.axis_size("inner")
    outer_count = lax.axis_size("outer")
    rank_grid = slab_rank.reshape(inner_count, outer_count)
    mine = lax.dynamic_index_in_dim(rank_grid, lax.axis_index("outer"), 1, keepdims=False)
    arrived = lax.all_to_all(pieces[None], "inner", split_axis=2, concat_axis=0, tiled=True)
    banded = composite(arrived, mine - jnp.min(mine))
    group_rank = jnp.min(rank_grid, axis=0) // inner_count
    arrived_groups = lax.all_to_all(banded[None], "outer", split_axis=3, concat_axis=0, tiled=True)
    total = composite(arrived_groups, group_rank)
    return jnp.concatenate([total[:3], 1.0 - total[3:]], axis=0)


ROWS = 16
COLS = 256
MESH = pl.DeviceIdType.MESH


def fused_kernel(
    inner_count, outer_count,
    density, extinction_in, occupancy_in, slope_in, rank_in, out,
    extinction, occupancy, slope, rank,
    field, fill, pieces, near, between_out, between, pair_out, pair, banded, groups,
    small_sem, load_sem, near_send, near_recv, between_send, between_recv,
    pair_send, pair_recv, outer_send, outer_recv,
):
    slices, height, width = field.shape
    band = height // inner_count
    chunks = band // ROWS
    part = width // outer_count
    me = lax.axis_index("inner")
    group = lax.axis_index("outer")

    chip, core = me // 2, me % 2
    sibling = chip * 2 + (1 - core)
    across = (1 - chip) * 2 + core
    diagonal = (1 - chip) * 2 + (1 - core)
    outer_partners = [lax.rem(group + step, outer_count) for step in range(1, outer_count)]

    def load(owner, chunk):
        rows = pl.ds(pl.multiple_of(owner * band + chunk * ROWS, ROWS), ROWS)
        return pltpu.make_async_copy(
            density.at[:, rows, :], field.at[:, rows, :], load_sem.at[owner, chunk]
        )

    small = [
        pltpu.make_async_copy(source, target, small_sem.at[index])
        for index, (source, target) in enumerate([
            (extinction_in, extinction), (occupancy_in, occupancy),
            (slope_in, slope), (rank_in, rank),
        ])
    ]
    for copy in small:
        copy.start()
    for chunk in range(chunks):
        for owner in (sibling, me, diagonal, across):
            load(owner, chunk).start()

    barrier = pltpu.get_barrier_semaphore()
    for partner in (sibling, across):
        pl.semaphore_signal(barrier, inc=1, device_id={"inner": partner}, device_id_type=MESH)
    for partner in outer_partners:
        pl.semaphore_signal(barrier, inc=1, device_id={"outer": partner}, device_id_type=MESH)
    for copy in small:
        copy.wait()

    block_rows, block_columns = occupancy.shape[1:]
    spread = (
        lax.broadcasted_iota(jnp.int32, (block_columns, width), 1) // (width // block_columns)
        == lax.broadcasted_iota(jnp.int32, (block_columns, width), 0)
    ).astype(jnp.float32)
    fill[...] = jnp.dot(
        occupancy[0].astype(jnp.float32), spread, preferred_element_type=jnp.float32
    )

    half = [slope[k] * 0.5 for k in range(3)]
    block_height = height // block_rows

    def march(owner, chunk):
        load(owner, chunk).wait()
        start = pl.multiple_of(owner * band + chunk * ROWS, ROWS)
        to = pl.ds(pl.multiple_of(chunk * ROWS, ROWS), ROWS)
        for column in range(0, width, COLS):
            columns = slice(column, column + COLS)
            through = jnp.ones((ROWS, COLS), jnp.float32)
            sums = [jnp.zeros((ROWS, COLS), jnp.float32) for k in range(3)]
            for t in range(slices):
                sample = field[t, pl.ds(start, ROWS), columns].astype(jnp.float32)
                after = through * jnp.exp2(sample * (extinction[t] * -1.4426950408889634))
                weight = through - after
                through = after
                shifted = sample - 0.3
                sums = [sums[k] + weight * jnp.tanh(half[k] * shifted) for k in range(3)]
            full = fill[pl.ds(start // block_height, 1), columns] > 0.5
            for k in range(3):
                pieces[owner, k, to, columns] = jnp.where(
                    full, 0.5 * ((1.0 - through) + sums[k]), 0.0
                )
            pieces[owner, 3, to, columns] = jnp.where(full, through, 1.0)

    def rows_of(chunk):
        return pl.ds(pl.multiple_of(chunk * ROWS, ROWS), ROWS)

    def copy_near(slot, chunk):
        return pltpu.make_async_remote_copy(
            src_ref=pieces.at[(sibling, diagonal)[slot], :, rows_of(chunk), :],
            dst_ref=near.at[slot, :, rows_of(chunk), :],
            send_sem=near_send.at[slot, chunk],
            recv_sem=near_recv.at[slot, chunk],
            device_id={"inner": sibling},
            device_id_type=MESH,
        )

    def copy_between(chunk):
        return pltpu.make_async_remote_copy(
            src_ref=between_out.at[rows_of(chunk), :],
            dst_ref=between.at[rows_of(chunk), :],
            send_sem=between_send.at[chunk],
            recv_sem=between_recv.at[chunk],
            device_id={"inner": across},
            device_id_type=MESH,
        )

    def copy_pair(chunk):
        return pltpu.make_async_remote_copy(
            src_ref=pair_out.at[:, rows_of(chunk), :],
            dst_ref=pair.at[:, rows_of(chunk), :],
            send_sem=pair_send.at[chunk],
            recv_sem=pair_recv.at[chunk],
            device_id={"inner": across},
            device_id_type=MESH,
        )

    def copy_outer(partner, slot, chunk):
        return pltpu.make_async_remote_copy(
            src_ref=banded.at[:, rows_of(chunk), pl.ds(pl.multiple_of(partner * part, 128), part)],
            dst_ref=groups.at[slot, :, rows_of(chunk), :],
            send_sem=outer_send.at[partner, chunk],
            recv_sem=outer_recv.at[slot, chunk],
            device_id={"outer": partner},
            device_id_type=MESH,
        )

    def rank_of(slab):
        return rank[slab * outer_count + group]

    mine_rank, near_rank = rank_of(me), rank_of(sibling)
    own_first = mine_rank < near_rank
    far_low = jnp.minimum(rank_of(across), rank_of(diagonal))
    far_high = jnp.maximum(rank_of(across), rank_of(diagonal))
    tiles = [slice(column, column + 128) for column in range(0, width, 128)]

    def inside(value):
        return (far_low < value) & (value < far_high)

    pl.semaphore_wait(barrier, 2 + len(outer_partners))

    @pl.loop(0, chunks)
    def _(chunk):
        rows = rows_of(chunk)
        march(sibling, chunk)
        copy_near(0, chunk).start()
        march(me, chunk)
        copy_near(0, chunk).wait_recv()
        for columns in tiles:
            between_out[rows, columns] = jnp.where(
                inside(mine_rank), pieces[me, 3, rows, columns], 1.0
            ) * jnp.where(inside(near_rank), near[0, 3, rows, columns], 1.0)
        copy_between(chunk).start()
        march(diagonal, chunk)
        copy_near(1, chunk).start()
        march(across, chunk)
        copy_near(1, chunk).wait_recv()
        copy_between(chunk).wait_recv()
        for columns in tiles:
            own = [pieces[across, k, rows, columns] for k in range(4)]
            other = [near[1, k, rows, columns] for k in range(4)]
            first = jnp.where(own_first, own[3], other[3])
            front = first * between[rows, columns]
            for k in range(3):
                pair_out[k, rows, columns] = jnp.where(
                    own_first, own[k] + front * other[k], other[k] + front * own[k]
                )
            pair_out[3, rows, columns] = first
            pair_out[4, rows, columns] = own[3] * other[3]
        copy_pair(chunk).start()

    @pl.loop(0, chunks)
    def _(chunk):
        copy_pair(chunk).wait_recv()
        rows = rows_of(chunk)
        for columns in tiles:
            own = [pieces[me, k, rows, columns] for k in range(4)]
            other = [near[0, k, rows, columns] for k in range(4)]
            far = [pair[k, rows, columns] for k in range(5)]

            def behind_far(value):
                return jnp.where(far_high < value, far[4], jnp.where(far_low < value, far[3], 1.0))

            own_front = behind_far(mine_rank) * jnp.where(own_first, 1.0, other[3])
            other_front = behind_far(near_rank) * jnp.where(own_first, own[3], 1.0)
            far_front = jnp.where(mine_rank < far_low, own[3], 1.0) * jnp.where(
                near_rank < far_low, other[3], 1.0
            )
            for k in range(3):
                banded[k, rows, columns] = (
                    own_front * own[k] + other_front * other[k] + far_front * far[k]
                )
            banded[3, rows, columns] = own[3] * other[3] * far[4]
        for partner in outer_partners:
            copy_outer(partner, group, chunk).start()

    ordered = outer_partners + [group]
    group_ranks = [rank[g] for g in ordered]
    mine = pl.ds(pl.multiple_of(group * part, 128), part)

    @pl.loop(0, chunks)
    def _(chunk):
        for partner in outer_partners:
            copy_outer(group, partner, chunk).wait_recv()
        rows = rows_of(chunk)

        def value(g, k):
            if g is group:
                return banded[k, rows, mine]
            return groups[g, k, rows, :]

        clear = [value(g, 3) for g in ordered]
        total = [0.0, 0.0, 0.0]
        for i, g in enumerate(ordered):
            front = 1.0
            for j in range(len(ordered)):
                if j != i:
                    front = front * jnp.where(group_ranks[j] < group_ranks[i], clear[j], 1.0)
            total = [total[k] + front * value(g, k) for k in range(3)]
        for k in range(3):
            out[k, rows, :] = total[k]
        through = clear[0]
        for other in clear[1:]:
            through = through * other
        out[3, rows, :] = 1.0 - through

    @pl.loop(0, chunks)
    def _(chunk):
        copy_near(0, chunk).wait_send()
        copy_near(1, chunk).wait_send()
        copy_between(chunk).wait_send()
        copy_pair(chunk).wait_send()
        for partner in outer_partners:
            copy_outer(partner, group, chunk).wait_send()


def fused(density, extinction, occupancy, colour_slope, slab_rank):
    inner_count = lax.axis_size("inner")
    outer_count = lax.axis_size("outer")
    slices, height, width = density.shape
    band, part = height // inner_count, width // outer_count
    chunks = band // ROWS
    vmem = pl.BlockSpec(memory_space=pltpu.VMEM)
    return pl.pallas_call(
        functools.partial(fused_kernel, inner_count, outer_count),
        out_shape=jax.ShapeDtypeStruct((4, band, part), jnp.float32),
        in_specs=[pl.BlockSpec(memory_space=pl.ANY)] * 5,
        out_specs=vmem,
        scratch_shapes=[
            pltpu.SMEM(extinction.shape, extinction.dtype),
            pltpu.VMEM(occupancy.shape, occupancy.dtype),
            pltpu.SMEM(colour_slope.shape, colour_slope.dtype),
            pltpu.SMEM(slab_rank.shape, slab_rank.dtype),
            pltpu.VMEM((slices, height, width), density.dtype),
            pltpu.VMEM((occupancy.shape[1], width), jnp.float32),
            pltpu.VMEM((inner_count, 4, band, width), jnp.float32),
            pltpu.VMEM((2, 4, band, width), jnp.float32),
            pltpu.VMEM((band, width), jnp.float32),
            pltpu.VMEM((band, width), jnp.float32),
            pltpu.VMEM((5, band, width), jnp.float32),
            pltpu.VMEM((5, band, width), jnp.float32),
            pltpu.VMEM((4, band, width), jnp.float32),
            pltpu.VMEM((outer_count, 4, band, part), jnp.float32),
            pltpu.SemaphoreType.DMA((4,)),
            pltpu.SemaphoreType.DMA((inner_count, chunks)),
            pltpu.SemaphoreType.DMA((2, chunks)),
            pltpu.SemaphoreType.DMA((2, chunks)),
            pltpu.SemaphoreType.DMA((chunks,)),
            pltpu.SemaphoreType.DMA((chunks,)),
            pltpu.SemaphoreType.DMA((chunks,)),
            pltpu.SemaphoreType.DMA((chunks,)),
            pltpu.SemaphoreType.DMA((outer_count, chunks)),
            pltpu.SemaphoreType.DMA((outer_count, chunks)),
        ],
        compiler_params=pltpu.CompilerParams(
            collective_id=0, has_side_effects=True, vmem_limit_bytes=60 * 2**20
        ),
    )(density, extinction, occupancy, colour_slope, slab_rank)


def solution(mesh):
    placed = (
        P(("inner", "outer"), None, "tile"),
        P(("inner", "outer")),
        P(("inner", "outer"), None, "tile"),
        P(),
        P(),
    )

    def local(density, *rest):
        part = density.shape[2] // mesh.shape["outer"]
        band = density.shape[1] // mesh.shape["inner"]
        whole = part % 128 == 0 and band % ROWS == 0 and mesh.shape["inner"] == 4
        return (fused if whole else shards)(density, *rest)

    return jax.shard_map(
        local,
        mesh=mesh,
        in_specs=placed,
        out_specs=P(None, "inner", ("tile", "outer")),
        check_vma=False,
    )
```

```python
import functools

import jax
import jax.numpy as jnp
from jax import lax
from jax.experimental import pallas as pl
from jax.experimental.pallas import tpu as pltpu
from jax.sharding import PartitionSpec as P


def march(density, extinction, occupancy, colour_slope):
    blocks = occupancy[0].astype(jnp.float32)
    filled = jnp.repeat(
        jnp.repeat(blocks, density.shape[1] // blocks.shape[0], axis=0),
        density.shape[2] // blocks.shape[1],
        axis=1,
    )

    def advance(carry, inputs):
        colour_sum, through = carry
        layer, absorb = inputs
        sample = layer.astype(jnp.float32) * filled
        opacity = 1.0 - jnp.exp(-absorb * sample)
        colour = jax.nn.sigmoid(colour_slope[:, None, None] * (sample - 0.3))
        colour_sum = colour_sum + (through * opacity)[None] * colour
        through = through * (1.0 - opacity)
        return ((colour_sum, through), None)

    start = (
        jnp.zeros((3,) + density.shape[1:], jnp.float32),
        jnp.ones(density.shape[1:], jnp.float32),
    )
    (colour_sum, through), unused = lax.scan(advance, start, (density, extinction))
    return jnp.concatenate([colour_sum, through[None]], axis=0)


def composite(pieces, ranks):
    count = pieces.shape[0]
    select = (ranks[None, :] == jnp.arange(count, dtype=jnp.int32)[:, None]).astype(jnp.float32)
    ordered = jnp.einsum("kj,jchw->kchw", select, pieces, precision=lax.Precision.HIGHEST)
    running = jnp.cumprod(ordered[:, 3], axis=0)
    front = jnp.concatenate([jnp.ones_like(running[:1]), running[:-1]], axis=0)
    colour = jnp.sum(ordered[:, :3] * front[:, None], axis=0)
    return jnp.concatenate([colour, running[-1:]], axis=0)


def shards(density, extinction, occupancy, colour_slope, slab_rank):
    pieces = march(density, extinction, occupancy, colour_slope)
    inner_count = lax.axis_size("inner")
    outer_count = lax.axis_size("outer")
    rank_grid = slab_rank.reshape(inner_count, outer_count)
    mine = lax.dynamic_index_in_dim(rank_grid, lax.axis_index("outer"), 1, keepdims=False)
    arrived = lax.all_to_all(pieces[None], "inner", split_axis=2, concat_axis=0, tiled=True)
    banded = composite(arrived, mine - jnp.min(mine))
    group_rank = jnp.min(rank_grid, axis=0) // inner_count
    arrived_groups = lax.all_to_all(banded[None], "outer", split_axis=3, concat_axis=0, tiled=True)
    total = composite(arrived_groups, group_rank)
    return jnp.concatenate([total[:3], 1.0 - total[3:]], axis=0)


ROWS = 16
COLS = 256
MESH = pl.DeviceIdType.MESH


def fused_kernel(
    inner_count, outer_count,
    density, extinction_in, occupancy_in, slope_in, rank_in, out,
    extinction, occupancy, slope, rank,
    field, fill, pieces, near, between_out, between, pair_out, pair, banded, groups,
    small_sem, load_sem, near_send, near_recv, between_send, between_recv,
    pair_send, pair_recv, outer_send, outer_recv,
):
    slices, height, width = field.shape
    band = height // inner_count
    chunks = band // ROWS
    part = width // outer_count
    me = lax.axis_index("inner")
    group = lax.axis_index("outer")

    chip, core = me // 2, me % 2
    sibling = chip * 2 + (1 - core)
    across = (1 - chip) * 2 + core
    diagonal = (1 - chip) * 2 + (1 - core)
    outer_partners = [lax.rem(group + step, outer_count) for step in range(1, outer_count)]

    def load(owner, chunk):
        rows = pl.ds(pl.multiple_of(owner * band + chunk * ROWS, ROWS), ROWS)
        return pltpu.make_async_copy(
            density.at[:, rows, :], field.at[:, rows, :], load_sem.at[owner, chunk]
        )

    small = [
        pltpu.make_async_copy(source, target, small_sem.at[index])
        for index, (source, target) in enumerate([
            (extinction_in, extinction), (occupancy_in, occupancy),
            (slope_in, slope), (rank_in, rank),
        ])
    ]
    for copy in small:
        copy.start()
    for owners in ((sibling, me), (diagonal, across)):
        for chunk in range(chunks):
            for owner in owners:
                load(owner, chunk).start()

    barrier = pltpu.get_barrier_semaphore()
    for partner in (sibling, across):
        pl.semaphore_signal(barrier, inc=1, device_id={"inner": partner}, device_id_type=MESH)
    for partner in outer_partners:
        pl.semaphore_signal(barrier, inc=1, device_id={"outer": partner}, device_id_type=MESH)
    for copy in small:
        copy.wait()

    block_rows, block_columns = occupancy.shape[1:]
    spread = (
        lax.broadcasted_iota(jnp.int32, (block_columns, width), 1) // (width // block_columns)
        == lax.broadcasted_iota(jnp.int32, (block_columns, width), 0)
    ).astype(jnp.float32)
    fill[...] = jnp.dot(
        occupancy[0].astype(jnp.float32), spread, preferred_element_type=jnp.float32
    )

    half = [slope[k] * 0.5 for k in range(3)]
    block_height = height // block_rows

    def march(owner, chunk):
        load(owner, chunk).wait()
        start = pl.multiple_of(owner * band + chunk * ROWS, ROWS)
        to = pl.ds(pl.multiple_of(chunk * ROWS, ROWS), ROWS)
        for column in range(0, width, COLS):
            columns = slice(column, column + COLS)
            through = jnp.ones((ROWS, COLS), jnp.float32)
            sums = [jnp.zeros((ROWS, COLS), jnp.float32) for k in range(3)]
            for t in range(slices):
                sample = field[t, pl.ds(start, ROWS), columns].astype(jnp.float32)
                after = through * jnp.exp2(sample * (extinction[t] * -1.4426950408889634))
                weight = through - after
                through = after
                shifted = sample - 0.3
                sums = [sums[k] + weight * jnp.tanh(half[k] * shifted) for k in range(3)]
            full = fill[pl.ds(start // block_height, 1), columns] > 0.5
            for k in range(3):
                pieces[owner, k, to, columns] = jnp.where(
                    full, 0.5 * ((1.0 - through) + sums[k]), 0.0
                )
            pieces[owner, 3, to, columns] = jnp.where(full, through, 1.0)

    def rows_of(chunk):
        return pl.ds(pl.multiple_of(chunk * ROWS, ROWS), ROWS)

    def copy_near(slot, chunk):
        return pltpu.make_async_remote_copy(
            src_ref=pieces.at[(sibling, diagonal)[slot], :, rows_of(chunk), :],
            dst_ref=near.at[slot, :, rows_of(chunk), :],
            send_sem=near_send.at[slot, chunk],
            recv_sem=near_recv.at[slot, chunk],
            device_id={"inner": sibling},
            device_id_type=MESH,
        )

    def copy_between(chunk):
        return pltpu.make_async_remote_copy(
            src_ref=between_out.at[rows_of(chunk), :],
            dst_ref=between.at[rows_of(chunk), :],
            send_sem=between_send.at[chunk],
            recv_sem=between_recv.at[chunk],
            device_id={"inner": across},
            device_id_type=MESH,
        )

    def copy_pair(chunk):
        return pltpu.make_async_remote_copy(
            src_ref=pair_out.at[:, rows_of(chunk), :],
            dst_ref=pair.at[:, rows_of(chunk), :],
            send_sem=pair_send.at[chunk],
            recv_sem=pair_recv.at[chunk],
            device_id={"inner": across},
            device_id_type=MESH,
        )

    def copy_outer(partner, slot, chunk):
        return pltpu.make_async_remote_copy(
            src_ref=banded.at[:, rows_of(chunk), pl.ds(pl.multiple_of(partner * part, 128), part)],
            dst_ref=groups.at[slot, :, rows_of(chunk), :],
            send_sem=outer_send.at[partner, chunk],
            recv_sem=outer_recv.at[slot, chunk],
            device_id={"outer": partner},
            device_id_type=MESH,
        )

    def rank_of(slab):
        return rank[slab * outer_count + group]

    mine_rank, near_rank = rank_of(me), rank_of(sibling)
    own_first = mine_rank < near_rank
    far_low = jnp.minimum(rank_of(across), rank_of(diagonal))
    far_high = jnp.maximum(rank_of(across), rank_of(diagonal))
    tiles = [slice(column, column + 128) for column in range(0, width, 128)]

    def inside(value):
        return (far_low < value) & (value < far_high)

    pl.semaphore_wait(barrier, 2 + len(outer_partners))

    def open_between(chunk):
        copy_near(0, chunk).wait_recv()
        rows = rows_of(chunk)
        for columns in tiles:
            between_out[rows, columns] = jnp.where(
                inside(mine_rank), pieces[me, 3, rows, columns], 1.0
            ) * jnp.where(inside(near_rank), near[0, 3, rows, columns], 1.0)
        copy_between(chunk).start()

    def merge_pair(chunk):
        copy_near(1, chunk).wait_recv()
        copy_between(chunk).wait_recv()
        rows = rows_of(chunk)
        for columns in tiles:
            own = [pieces[across, k, rows, columns] for k in range(4)]
            other = [near[1, k, rows, columns] for k in range(4)]
            first = jnp.where(own_first, own[3], other[3])
            front = first * between[rows, columns]
            for k in range(3):
                pair_out[k, rows, columns] = jnp.where(
                    own_first, own[k] + front * other[k], other[k] + front * own[k]
                )
            pair_out[3, rows, columns] = first
            pair_out[4, rows, columns] = own[3] * other[3]
        copy_pair(chunk).start()

    @pl.loop(0, chunks + 1)
    def _(chunk):
        @pl.when(chunk < chunks)
        def _():
            march(sibling, chunk)
            copy_near(0, chunk).start()
            march(me, chunk)

        @pl.when(chunk >= 1)
        def _():
            open_between(chunk - 1)

    @pl.loop(0, chunks + 1)
    def _(chunk):
        @pl.when(chunk < chunks)
        def _():
            march(diagonal, chunk)
            copy_near(1, chunk).start()
            march(across, chunk)

        @pl.when(chunk >= 1)
        def _():
            merge_pair(chunk - 1)

    @pl.loop(0, chunks)
    def _(chunk):
        copy_pair(chunk).wait_recv()
        rows = rows_of(chunk)
        for columns in tiles:
            own = [pieces[me, k, rows, columns] for k in range(4)]
            other = [near[0, k, rows, columns] for k in range(4)]
            far = [pair[k, rows, columns] for k in range(5)]

            def behind_far(value):
                return jnp.where(far_high < value, far[4], jnp.where(far_low < value, far[3], 1.0))

            own_front = behind_far(mine_rank) * jnp.where(own_first, 1.0, other[3])
            other_front = behind_far(near_rank) * jnp.where(own_first, own[3], 1.0)
            far_front = jnp.where(mine_rank < far_low, own[3], 1.0) * jnp.where(
                near_rank < far_low, other[3], 1.0
            )
            for k in range(3):
                banded[k, rows, columns] = (
                    own_front * own[k] + other_front * other[k] + far_front * far[k]
                )
            banded[3, rows, columns] = own[3] * other[3] * far[4]
        for partner in outer_partners:
            copy_outer(partner, group, chunk).start()

    ordered = outer_partners + [group]
    group_ranks = [rank[g] for g in ordered]
    mine = pl.ds(pl.multiple_of(group * part, 128), part)

    @pl.loop(0, chunks)
    def _(chunk):
        for partner in outer_partners:
            copy_outer(group, partner, chunk).wait_recv()
        rows = rows_of(chunk)

        def value(g, k):
            if g is group:
                return banded[k, rows, mine]
            return groups[g, k, rows, :]

        clear = [value(g, 3) for g in ordered]
        total = [0.0, 0.0, 0.0]
        for i, g in enumerate(ordered):
            front = 1.0
            for j in range(len(ordered)):
                if j != i:
                    front = front * jnp.where(group_ranks[j] < group_ranks[i], clear[j], 1.0)
            total = [total[k] + front * value(g, k) for k in range(3)]
        for k in range(3):
            out[k, rows, :] = total[k]
        through = clear[0]
        for other in clear[1:]:
            through = through * other
        out[3, rows, :] = 1.0 - through

    @pl.loop(0, chunks)
    def _(chunk):
        copy_near(0, chunk).wait_send()
        copy_near(1, chunk).wait_send()
        copy_between(chunk).wait_send()
        copy_pair(chunk).wait_send()
        for partner in outer_partners:
            copy_outer(partner, group, chunk).wait_send()


def fused(density, extinction, occupancy, colour_slope, slab_rank):
    inner_count = lax.axis_size("inner")
    outer_count = lax.axis_size("outer")
    slices, height, width = density.shape
    band, part = height // inner_count, width // outer_count
    chunks = band // ROWS
    vmem = pl.BlockSpec(memory_space=pltpu.VMEM)
    return pl.pallas_call(
        functools.partial(fused_kernel, inner_count, outer_count),
        out_shape=jax.ShapeDtypeStruct((4, band, part), jnp.float32),
        in_specs=[pl.BlockSpec(memory_space=pl.ANY)] * 5,
        out_specs=vmem,
        scratch_shapes=[
            pltpu.SMEM(extinction.shape, extinction.dtype),
            pltpu.VMEM(occupancy.shape, occupancy.dtype),
            pltpu.SMEM(colour_slope.shape, colour_slope.dtype),
            pltpu.SMEM(slab_rank.shape, slab_rank.dtype),
            pltpu.VMEM((slices, height, width), density.dtype),
            pltpu.VMEM((occupancy.shape[1], width), jnp.float32),
            pltpu.VMEM((inner_count, 4, band, width), jnp.float32),
            pltpu.VMEM((2, 4, band, width), jnp.float32),
            pltpu.VMEM((band, width), jnp.float32),
            pltpu.VMEM((band, width), jnp.float32),
            pltpu.VMEM((5, band, width), jnp.float32),
            pltpu.VMEM((5, band, width), jnp.float32),
            pltpu.VMEM((4, band, width), jnp.float32),
            pltpu.VMEM((outer_count, 4, band, part), jnp.float32),
            pltpu.SemaphoreType.DMA((4,)),
            pltpu.SemaphoreType.DMA((inner_count, chunks)),
            pltpu.SemaphoreType.DMA((2, chunks)),
            pltpu.SemaphoreType.DMA((2, chunks)),
            pltpu.SemaphoreType.DMA((chunks,)),
            pltpu.SemaphoreType.DMA((chunks,)),
            pltpu.SemaphoreType.DMA((chunks,)),
            pltpu.SemaphoreType.DMA((chunks,)),
            pltpu.SemaphoreType.DMA((outer_count, chunks)),
            pltpu.SemaphoreType.DMA((outer_count, chunks)),
        ],
        compiler_params=pltpu.CompilerParams(
            collective_id=0, has_side_effects=True, vmem_limit_bytes=60 * 2**20
        ),
    )(density, extinction, occupancy, colour_slope, slab_rank)


def solution(mesh):
    placed = (
        P(("inner", "outer"), None, "tile"),
        P(("inner", "outer")),
        P(("inner", "outer"), None, "tile"),
        P(),
        P(),
    )

    def local(density, *rest):
        part = density.shape[2] // mesh.shape["outer"]
        band = density.shape[1] // mesh.shape["inner"]
        whole = part % 128 == 0 and band % ROWS == 0 and mesh.shape["inner"] == 4
        return (fused if whole else shards)(density, *rest)

    return jax.shard_map(
        local,
        mesh=mesh,
        in_specs=placed,
        out_specs=P(None, "inner", ("tile", "outer")),
        check_vma=False,
    )
```

```python
import functools

import jax
import jax.numpy as jnp
from jax import lax
from jax.experimental import pallas as pl
from jax.experimental.pallas import tpu as pltpu
from jax.sharding import PartitionSpec as P


def march(density, extinction, occupancy, colour_slope):
    blocks = occupancy[0].astype(jnp.float32)
    filled = jnp.repeat(
        jnp.repeat(blocks, density.shape[1] // blocks.shape[0], axis=0),
        density.shape[2] // blocks.shape[1],
        axis=1,
    )

    def advance(carry, inputs):
        colour_sum, through = carry
        layer, absorb = inputs
        sample = layer.astype(jnp.float32) * filled
        opacity = 1.0 - jnp.exp(-absorb * sample)
        colour = jax.nn.sigmoid(colour_slope[:, None, None] * (sample - 0.3))
        colour_sum = colour_sum + (through * opacity)[None] * colour
        through = through * (1.0 - opacity)
        return ((colour_sum, through), None)

    start = (
        jnp.zeros((3,) + density.shape[1:], jnp.float32),
        jnp.ones(density.shape[1:], jnp.float32),
    )
    (colour_sum, through), unused = lax.scan(advance, start, (density, extinction))
    return jnp.concatenate([colour_sum, through[None]], axis=0)


def composite(pieces, ranks):
    count = pieces.shape[0]
    select = (ranks[None, :] == jnp.arange(count, dtype=jnp.int32)[:, None]).astype(jnp.float32)
    ordered = jnp.einsum("kj,jchw->kchw", select, pieces, precision=lax.Precision.HIGHEST)
    running = jnp.cumprod(ordered[:, 3], axis=0)
    front = jnp.concatenate([jnp.ones_like(running[:1]), running[:-1]], axis=0)
    colour = jnp.sum(ordered[:, :3] * front[:, None], axis=0)
    return jnp.concatenate([colour, running[-1:]], axis=0)


def shards(density, extinction, occupancy, colour_slope, slab_rank):
    pieces = march(density, extinction, occupancy, colour_slope)
    inner_count = lax.axis_size("inner")
    outer_count = lax.axis_size("outer")
    rank_grid = slab_rank.reshape(inner_count, outer_count)
    mine = lax.dynamic_index_in_dim(rank_grid, lax.axis_index("outer"), 1, keepdims=False)
    arrived = lax.all_to_all(pieces[None], "inner", split_axis=2, concat_axis=0, tiled=True)
    banded = composite(arrived, mine - jnp.min(mine))
    group_rank = jnp.min(rank_grid, axis=0) // inner_count
    arrived_groups = lax.all_to_all(banded[None], "outer", split_axis=3, concat_axis=0, tiled=True)
    total = composite(arrived_groups, group_rank)
    return jnp.concatenate([total[:3], 1.0 - total[3:]], axis=0)


ROWS = 16
PIECE = 8
COLS = 256
MESH = pl.DeviceIdType.MESH


def fused_kernel(
    inner_count, outer_count,
    density, extinction_in, occupancy_in, slope_in, rank_in, out,
    extinction, occupancy, slope, rank,
    field, fill, pieces, raw, near, between_out, between, pair_out, pair, banded, groups,
    small_sem, load_sem, raw_send, raw_recv, near_send, near_recv, between_send, between_recv,
    pair_send, pair_recv, outer_send, outer_recv,
):
    slices, height, width = field.shape
    band = height // inner_count
    chunks = band // ROWS
    part = width // outer_count
    per_chunk = ROWS // PIECE
    me = lax.axis_index("inner")
    group = lax.axis_index("outer")

    chip, core = me // 2, me % 2
    sibling = chip * 2 + (1 - core)
    across = (1 - chip) * 2 + core
    diagonal = (1 - chip) * 2 + (1 - core)
    outer_partners = [lax.rem(group + step, outer_count) for step in range(1, outer_count)]

    def load(owner, chunk):
        rows = pl.ds(pl.multiple_of(owner * band + chunk * ROWS, ROWS), ROWS)
        return pltpu.make_async_copy(
            density.at[:, rows, :], field.at[:, rows, :], load_sem.at[owner, chunk]
        )

    small = [
        pltpu.make_async_copy(source, target, small_sem.at[index])
        for index, (source, target) in enumerate([
            (extinction_in, extinction), (occupancy_in, occupancy),
            (slope_in, slope), (rank_in, rank),
        ])
    ]
    for copy in small:
        copy.start()
    order = [(owner, 0) for owner in (across, diagonal)]
    order += [(owner, chunk) for chunk in range(chunks) for owner in (sibling, me)]
    order += [(owner, chunk) for chunk in range(1, chunks) for owner in (diagonal, across)]
    for owner, chunk in order:
        load(owner, chunk).start()

    barrier = pltpu.get_barrier_semaphore()
    for partner in (sibling, across, diagonal):
        pl.semaphore_signal(barrier, inc=1, device_id={"inner": partner}, device_id_type=MESH)
    for partner in outer_partners:
        pl.semaphore_signal(barrier, inc=1, device_id={"outer": partner}, device_id_type=MESH)
    for copy in small:
        copy.wait()

    block_rows, block_columns = occupancy.shape[1:]
    spread = (
        lax.broadcasted_iota(jnp.int32, (block_columns, width), 1) // (width // block_columns)
        == lax.broadcasted_iota(jnp.int32, (block_columns, width), 0)
    ).astype(jnp.float32)
    fill[...] = jnp.dot(
        occupancy[0].astype(jnp.float32), spread, preferred_element_type=jnp.float32
    )

    half = [slope[k] * 0.5 for k in range(3)]
    block_height = height // block_rows

    def march(owner, chunk):
        load(owner, chunk).wait()
        start = pl.multiple_of(owner * band + chunk * ROWS, ROWS)
        to = pl.ds(pl.multiple_of(chunk * ROWS, ROWS), ROWS)
        for column in range(0, width, COLS):
            columns = slice(column, column + COLS)
            through = jnp.ones((ROWS, COLS), jnp.float32)
            sums = [jnp.zeros((ROWS, COLS), jnp.float32) for k in range(3)]
            for t in range(slices):
                sample = field[t, pl.ds(start, ROWS), columns].astype(jnp.float32)
                after = through * jnp.exp2(sample * (extinction[t] * -1.4426950408889634))
                weight = through - after
                through = after
                shifted = sample - 0.3
                sums = [sums[k] + weight * jnp.tanh(half[k] * shifted) for k in range(3)]
            full = fill[pl.ds(start // block_height, 1), columns] > 0.5
            for k in range(3):
                pieces[owner, k, to, columns] = jnp.where(
                    full, 0.5 * ((1.0 - through) + sums[k]), 0.0
                )
            pieces[owner, 3, to, columns] = jnp.where(full, through, 1.0)

    def rows_of(chunk):
        return pl.ds(pl.multiple_of(chunk * ROWS, ROWS), ROWS)

    def piece_rows(piece):
        return pl.ds(pl.multiple_of(piece * PIECE, PIECE), PIECE)

    def copy_raw(slot):
        partner = (across, diagonal)[slot]
        return pltpu.make_async_remote_copy(
            src_ref=pieces.at[partner, :, rows_of(0), :],
            dst_ref=raw.at[slot],
            send_sem=raw_send.at[slot],
            recv_sem=raw_recv.at[slot],
            device_id={"inner": partner},
            device_id_type=MESH,
        )

    def copy_near(slot, chunk):
        return pltpu.make_async_remote_copy(
            src_ref=pieces.at[(sibling, diagonal)[slot], :, rows_of(chunk), :],
            dst_ref=near.at[slot, :, rows_of(chunk), :],
            send_sem=near_send.at[slot, chunk],
            recv_sem=near_recv.at[slot, chunk],
            device_id={"inner": sibling},
            device_id_type=MESH,
        )

    def copy_between(chunk):
        return pltpu.make_async_remote_copy(
            src_ref=between_out.at[rows_of(chunk), :],
            dst_ref=between.at[rows_of(chunk), :],
            send_sem=between_send.at[chunk],
            recv_sem=between_recv.at[chunk],
            device_id={"inner": across},
            device_id_type=MESH,
        )

    def copy_pair(piece):
        return pltpu.make_async_remote_copy(
            src_ref=pair_out.at[:, piece_rows(piece), :],
            dst_ref=pair.at[:, piece_rows(piece), :],
            send_sem=pair_send.at[piece],
            recv_sem=pair_recv.at[piece],
            device_id={"inner": across},
            device_id_type=MESH,
        )

    def copy_outer(partner, slot, piece):
        columns = pl.ds(pl.multiple_of(partner * part, 128), part)
        return pltpu.make_async_remote_copy(
            src_ref=banded.at[:, piece_rows(piece), columns],
            dst_ref=groups.at[slot, :, piece_rows(piece), :],
            send_sem=outer_send.at[partner, piece],
            recv_sem=outer_recv.at[slot, piece],
            device_id={"outer": partner},
            device_id_type=MESH,
        )

    def rank_of(slab):
        return rank[slab * outer_count + group]

    mine_rank, near_rank = rank_of(me), rank_of(sibling)
    own_first = mine_rank < near_rank
    far_low = jnp.minimum(rank_of(across), rank_of(diagonal))
    far_high = jnp.maximum(rank_of(across), rank_of(diagonal))
    tiles = [slice(column, column + 128) for column in range(0, width, 128)]

    def inside(value):
        return (far_low < value) & (value < far_high)


    def open_between(chunk):
        copy_near(0, chunk).wait_recv()
        rows = rows_of(chunk)
        for columns in tiles:
            between_out[rows, columns] = jnp.where(
                inside(mine_rank), pieces[me, 3, rows, columns], 1.0
            ) * jnp.where(inside(near_rank), near[0, 3, rows, columns], 1.0)
        copy_between(chunk).start()

    def merge_pair(chunk):
        copy_near(1, chunk).wait_recv()
        copy_between(chunk).wait_recv()
        rows = rows_of(chunk)
        for columns in tiles:
            own = [pieces[across, k, rows, columns] for k in range(4)]
            other = [near[1, k, rows, columns] for k in range(4)]
            first = jnp.where(own_first, own[3], other[3])
            front = first * between[rows, columns]
            for k in range(3):
                pair_out[k, rows, columns] = jnp.where(
                    own_first, own[k] + front * other[k], other[k] + front * own[k]
                )
            pair_out[3, rows, columns] = first
            pair_out[4, rows, columns] = own[3] * other[3]
        for piece in range(per_chunk):
            copy_pair(chunk * per_chunk + piece).start()

    march(across, 0)
    march(diagonal, 0)
    pl.semaphore_wait(barrier, 3 + len(outer_partners))
    copy_raw(0).start()
    copy_raw(1).start()

    @pl.loop(0, chunks + 1)
    def _(chunk):
        @pl.when(chunk < chunks)
        def _():
            march(sibling, chunk)
            copy_near(0, chunk).start()
            march(me, chunk)

        @pl.when(chunk >= 2)
        def _():
            open_between(chunk - 1)

    @pl.loop(1, chunks + 1)
    def _(chunk):
        @pl.when(chunk < chunks)
        def _():
            march(diagonal, chunk)
            copy_near(1, chunk).start()
            march(across, chunk)

        @pl.when(chunk >= 2)
        def _():
            merge_pair(chunk - 1)

    def merge_raw():
        copy_near(0, 0).wait_recv()
        copy_raw(0).wait_recv()
        copy_raw(1).wait_recv()
        rows = rows_of(0)
        across_first = rank_of(across) < rank_of(diagonal)
        for columns in tiles:
            one = [raw[0, k, :, columns] for k in range(4)]
            other = [raw[1, k, :, columns] for k in range(4)]
            first = jnp.where(across_first, one[3], other[3])
            front = first * jnp.where(
                inside(mine_rank), pieces[me, 3, rows, columns], 1.0
            ) * jnp.where(inside(near_rank), near[0, 3, rows, columns], 1.0)
            for k in range(3):
                pair[k, rows, columns] = jnp.where(
                    across_first, one[k] + front * other[k], other[k] + front * one[k]
                )
            pair[3, rows, columns] = first
            pair[4, rows, columns] = one[3] * other[3]

    def composite(piece):
        rows = piece_rows(piece)
        for columns in tiles:
            own = [pieces[me, k, rows, columns] for k in range(4)]
            other = [near[0, k, rows, columns] for k in range(4)]
            far = [pair[k, rows, columns] for k in range(5)]

            def behind_far(value):
                return jnp.where(far_high < value, far[4], jnp.where(far_low < value, far[3], 1.0))

            own_front = behind_far(mine_rank) * jnp.where(own_first, 1.0, other[3])
            other_front = behind_far(near_rank) * jnp.where(own_first, own[3], 1.0)
            far_front = jnp.where(mine_rank < far_low, own[3], 1.0) * jnp.where(
                near_rank < far_low, other[3], 1.0
            )
            for k in range(3):
                banded[k, rows, columns] = (
                    own_front * own[k] + other_front * other[k] + far_front * far[k]
                )
            banded[3, rows, columns] = own[3] * other[3] * far[4]
        for partner in outer_partners:
            copy_outer(partner, group, piece).start()

    merge_raw()

    @pl.loop(0, per_chunk)
    def _(piece):
        composite(piece)

    @pl.loop(per_chunk, chunks * per_chunk)
    def _(piece):
        copy_pair(piece).wait_recv()
        composite(piece)

    ordered = outer_partners + [group]
    group_ranks = [rank[g] for g in ordered]
    mine = pl.ds(pl.multiple_of(group * part, 128), part)

    @pl.loop(0, chunks * per_chunk)
    def _(piece):
        for partner in outer_partners:
            copy_outer(group, partner, piece).wait_recv()
        rows = piece_rows(piece)

        def value(g, k):
            if g is group:
                return banded[k, rows, mine]
            return groups[g, k, rows, :]

        clear = [value(g, 3) for g in ordered]
        total = [0.0, 0.0, 0.0]
        for i, g in enumerate(ordered):
            front = 1.0
            for j in range(len(ordered)):
                if j != i:
                    front = front * jnp.where(group_ranks[j] < group_ranks[i], clear[j], 1.0)
            total = [total[k] + front * value(g, k) for k in range(3)]
        for k in range(3):
            out[k, rows, :] = total[k]
        through = clear[0]
        for other in clear[1:]:
            through = through * other
        out[3, rows, :] = 1.0 - through

    copy_raw(0).wait_send()
    copy_raw(1).wait_send()
    copy_near(0, 0).wait_send()

    @pl.loop(1, chunks)
    def _(chunk):
        copy_near(0, chunk).wait_send()
        copy_near(1, chunk).wait_send()
        copy_between(chunk).wait_send()
        for piece in range(per_chunk):
            copy_pair(chunk * per_chunk + piece).wait_send()

    @pl.loop(0, chunks * per_chunk)
    def _(piece):
        for partner in outer_partners:
            copy_outer(partner, group, piece).wait_send()


def fused(density, extinction, occupancy, colour_slope, slab_rank):
    inner_count = lax.axis_size("inner")
    outer_count = lax.axis_size("outer")
    slices, height, width = density.shape
    band, part = height // inner_count, width // outer_count
    chunks = band // ROWS
    vmem = pl.BlockSpec(memory_space=pltpu.VMEM)
    return pl.pallas_call(
        functools.partial(fused_kernel, inner_count, outer_count),
        out_shape=jax.ShapeDtypeStruct((4, band, part), jnp.float32),
        in_specs=[pl.BlockSpec(memory_space=pl.ANY)] * 5,
        out_specs=vmem,
        scratch_shapes=[
            pltpu.SMEM(extinction.shape, extinction.dtype),
            pltpu.VMEM(occupancy.shape, occupancy.dtype),
            pltpu.SMEM(colour_slope.shape, colour_slope.dtype),
            pltpu.SMEM(slab_rank.shape, slab_rank.dtype),
            pltpu.VMEM((slices, height, width), density.dtype),
            pltpu.VMEM((occupancy.shape[1], width), jnp.float32),
            pltpu.VMEM((inner_count, 4, band, width), jnp.float32),
            pltpu.VMEM((2, 4, ROWS, width), jnp.float32),
            pltpu.VMEM((2, 4, band, width), jnp.float32),
            pltpu.VMEM((band, width), jnp.float32),
            pltpu.VMEM((band, width), jnp.float32),
            pltpu.VMEM((5, band, width), jnp.float32),
            pltpu.VMEM((5, band, width), jnp.float32),
            pltpu.VMEM((4, band, width), jnp.float32),
            pltpu.VMEM((outer_count, 4, band, part), jnp.float32),
            pltpu.SemaphoreType.DMA((4,)),
            pltpu.SemaphoreType.DMA((inner_count, chunks)),
            pltpu.SemaphoreType.DMA((2,)),
            pltpu.SemaphoreType.DMA((2,)),
            pltpu.SemaphoreType.DMA((2, chunks)),
            pltpu.SemaphoreType.DMA((2, chunks)),
            pltpu.SemaphoreType.DMA((chunks,)),
            pltpu.SemaphoreType.DMA((chunks,)),
            pltpu.SemaphoreType.DMA((chunks * ROWS // PIECE,)),
            pltpu.SemaphoreType.DMA((chunks * ROWS // PIECE,)),
            pltpu.SemaphoreType.DMA((outer_count, chunks * ROWS // PIECE)),
            pltpu.SemaphoreType.DMA((outer_count, chunks * ROWS // PIECE)),
        ],
        compiler_params=pltpu.CompilerParams(
            collective_id=0, has_side_effects=True, vmem_limit_bytes=60 * 2**20
        ),
    )(density, extinction, occupancy, colour_slope, slab_rank)


def solution(mesh):
    placed = (
        P(("inner", "outer"), None, "tile"),
        P(("inner", "outer")),
        P(("inner", "outer"), None, "tile"),
        P(),
        P(),
    )

    def local(density, *rest):
        part = density.shape[2] // mesh.shape["outer"]
        band = density.shape[1] // mesh.shape["inner"]
        whole = part % 128 == 0 and band % ROWS == 0 and mesh.shape["inner"] == 4
        return (fused if whole else shards)(density, *rest)

    return jax.shard_map(
        local,
        mesh=mesh,
        in_specs=placed,
        out_specs=P(None, "inner", ("tile", "outer")),
        check_vma=False,
    )
```

```python
import functools

import jax
import jax.numpy as jnp
from jax import lax
from jax.experimental import pallas as pl
from jax.experimental.pallas import tpu as pltpu
from jax.sharding import PartitionSpec as P


def march(density, extinction, occupancy, colour_slope):
    blocks = occupancy[0].astype(jnp.float32)
    filled = jnp.repeat(
        jnp.repeat(blocks, density.shape[1] // blocks.shape[0], axis=0),
        density.shape[2] // blocks.shape[1],
        axis=1,
    )

    def advance(carry, inputs):
        colour_sum, through = carry
        layer, absorb = inputs
        sample = layer.astype(jnp.float32) * filled
        opacity = 1.0 - jnp.exp(-absorb * sample)
        colour = jax.nn.sigmoid(colour_slope[:, None, None] * (sample - 0.3))
        colour_sum = colour_sum + (through * opacity)[None] * colour
        through = through * (1.0 - opacity)
        return ((colour_sum, through), None)

    start = (
        jnp.zeros((3,) + density.shape[1:], jnp.float32),
        jnp.ones(density.shape[1:], jnp.float32),
    )
    (colour_sum, through), unused = lax.scan(advance, start, (density, extinction))
    return jnp.concatenate([colour_sum, through[None]], axis=0)


def composite(pieces, ranks):
    count = pieces.shape[0]
    select = (ranks[None, :] == jnp.arange(count, dtype=jnp.int32)[:, None]).astype(jnp.float32)
    ordered = jnp.einsum("kj,jchw->kchw", select, pieces, precision=lax.Precision.HIGHEST)
    running = jnp.cumprod(ordered[:, 3], axis=0)
    front = jnp.concatenate([jnp.ones_like(running[:1]), running[:-1]], axis=0)
    colour = jnp.sum(ordered[:, :3] * front[:, None], axis=0)
    return jnp.concatenate([colour, running[-1:]], axis=0)


def shards(density, extinction, occupancy, colour_slope, slab_rank):
    pieces = march(density, extinction, occupancy, colour_slope)
    inner_count = lax.axis_size("inner")
    outer_count = lax.axis_size("outer")
    rank_grid = slab_rank.reshape(inner_count, outer_count)
    mine = lax.dynamic_index_in_dim(rank_grid, lax.axis_index("outer"), 1, keepdims=False)
    arrived = lax.all_to_all(pieces[None], "inner", split_axis=2, concat_axis=0, tiled=True)
    banded = composite(arrived, mine - jnp.min(mine))
    group_rank = jnp.min(rank_grid, axis=0) // inner_count
    arrived_groups = lax.all_to_all(banded[None], "outer", split_axis=3, concat_axis=0, tiled=True)
    total = composite(arrived_groups, group_rank)
    return jnp.concatenate([total[:3], 1.0 - total[3:]], axis=0)


ROWS = 16
PIECE = 8
LAG = 2
COLS = 256
MESH = pl.DeviceIdType.MESH


def fused_kernel(
    inner_count, outer_count,
    density, extinction_in, occupancy_in, slope_in, rank_in, out,
    extinction, occupancy, slope, rank,
    field, fill, pieces, raw, near, between_out, between, pair_out, pair, banded, groups,
    small_sem, load_sem, raw_send, raw_recv, near_send, near_recv, between_send, between_recv,
    pair_send, pair_recv, outer_send, outer_recv,
):
    slices, height, width = field.shape
    band = height // inner_count
    chunks = band // ROWS
    part = width // outer_count
    per_chunk = ROWS // PIECE
    me = lax.axis_index("inner")
    group = lax.axis_index("outer")

    chip, core = me // 2, me % 2
    sibling = chip * 2 + (1 - core)
    across = (1 - chip) * 2 + core
    diagonal = (1 - chip) * 2 + (1 - core)
    outer_partners = [lax.rem(group + step, outer_count) for step in range(1, outer_count)]

    def load(owner, chunk):
        rows = pl.ds(pl.multiple_of(owner * band + chunk * ROWS, ROWS), ROWS)
        return pltpu.make_async_copy(
            density.at[:, rows, :], field.at[:, rows, :], load_sem.at[owner, chunk]
        )

    barrier = pltpu.get_barrier_semaphore()
    for partner in (sibling, across, diagonal):
        pl.semaphore_signal(barrier, inc=1, device_id={"inner": partner}, device_id_type=MESH)
    for partner in outer_partners:
        pl.semaphore_signal(barrier, inc=1, device_id={"outer": partner}, device_id_type=MESH)
    small = [
        pltpu.make_async_copy(source, target, small_sem.at[index])
        for index, (source, target) in enumerate([
            (extinction_in, extinction), (occupancy_in, occupancy),
            (slope_in, slope), (rank_in, rank),
        ])
    ]
    for copy in small:
        copy.start()
    order = [(owner, 0) for owner in (across, diagonal)]
    order += [(owner, chunk) for chunk in range(chunks) for owner in (sibling, me)]
    order += [(owner, chunk) for chunk in range(1, chunks) for owner in (diagonal, across)]
    for owner, chunk in order[:2]:
        load(owner, chunk).start()

    for copy in small:
        copy.wait()

    block_rows, block_columns = occupancy.shape[1:]
    spread = (
        lax.broadcasted_iota(jnp.int32, (block_columns, width), 1) // (width // block_columns)
        == lax.broadcasted_iota(jnp.int32, (block_columns, width), 0)
    ).astype(jnp.float32)
    fill[...] = jnp.dot(
        occupancy[0].astype(jnp.float32), spread, preferred_element_type=jnp.float32
    )

    half = [slope[k] * 0.5 for k in range(3)]
    block_height = height // block_rows

    def march(owner, chunk):
        load(owner, chunk).wait()
        start = pl.multiple_of(owner * band + chunk * ROWS, ROWS)
        to = pl.ds(pl.multiple_of(chunk * ROWS, ROWS), ROWS)
        for column in range(0, width, COLS):
            columns = slice(column, column + COLS)
            through = jnp.ones((ROWS, COLS), jnp.float32)
            sums = [jnp.zeros((ROWS, COLS), jnp.float32) for k in range(3)]
            for t in range(slices):
                sample = field[t, pl.ds(start, ROWS), columns].astype(jnp.float32)
                after = through * jnp.exp2(sample * (extinction[t] * -1.4426950408889634))
                weight = through - after
                through = after
                shifted = sample - 0.3
                sums = [sums[k] + weight * jnp.tanh(half[k] * shifted) for k in range(3)]
            full = fill[pl.ds(start // block_height, 1), columns] > 0.5
            for k in range(3):
                pieces[owner, k, to, columns] = jnp.where(
                    full, 0.5 * ((1.0 - through) + sums[k]), 0.0
                )
            pieces[owner, 3, to, columns] = jnp.where(full, through, 1.0)

    def rows_of(chunk):
        return pl.ds(pl.multiple_of(chunk * ROWS, ROWS), ROWS)

    def piece_rows(piece):
        return pl.ds(pl.multiple_of(piece * PIECE, PIECE), PIECE)

    def copy_raw(slot):
        partner = (across, diagonal)[slot]
        return pltpu.make_async_remote_copy(
            src_ref=pieces.at[partner, :, rows_of(0), :],
            dst_ref=raw.at[slot],
            send_sem=raw_send.at[slot],
            recv_sem=raw_recv.at[slot],
            device_id={"inner": partner},
            device_id_type=MESH,
        )

    def copy_near(slot, chunk):
        return pltpu.make_async_remote_copy(
            src_ref=pieces.at[(sibling, diagonal)[slot], :, rows_of(chunk), :],
            dst_ref=near.at[slot, :, rows_of(chunk), :],
            send_sem=near_send.at[slot, chunk],
            recv_sem=near_recv.at[slot, chunk],
            device_id={"inner": sibling},
            device_id_type=MESH,
        )

    def copy_between(chunk):
        return pltpu.make_async_remote_copy(
            src_ref=between_out.at[rows_of(chunk), :],
            dst_ref=between.at[rows_of(chunk), :],
            send_sem=between_send.at[chunk],
            recv_sem=between_recv.at[chunk],
            device_id={"inner": across},
            device_id_type=MESH,
        )

    def copy_pair(piece):
        return pltpu.make_async_remote_copy(
            src_ref=pair_out.at[:, piece_rows(piece), :],
            dst_ref=pair.at[:, piece_rows(piece), :],
            send_sem=pair_send.at[piece],
            recv_sem=pair_recv.at[piece],
            device_id={"inner": across},
            device_id_type=MESH,
        )

    def copy_outer(partner, slot, piece):
        columns = pl.ds(pl.multiple_of(partner * part, 128), part)
        return pltpu.make_async_remote_copy(
            src_ref=banded.at[:, piece_rows(piece), columns],
            dst_ref=groups.at[slot, :, piece_rows(piece), :],
            send_sem=outer_send.at[partner, piece],
            recv_sem=outer_recv.at[slot, piece],
            device_id={"outer": partner},
            device_id_type=MESH,
        )

    def rank_of(slab):
        return rank[slab * outer_count + group]

    mine_rank, near_rank = rank_of(me), rank_of(sibling)
    own_first = mine_rank < near_rank
    far_low = jnp.minimum(rank_of(across), rank_of(diagonal))
    far_high = jnp.maximum(rank_of(across), rank_of(diagonal))
    tiles = [slice(column, column + 128) for column in range(0, width, 128)]

    def inside(value):
        return (far_low < value) & (value < far_high)


    def open_between(chunk):
        copy_near(0, chunk).wait_recv()
        rows = rows_of(chunk)
        for columns in tiles:
            between_out[rows, columns] = jnp.where(
                inside(mine_rank), pieces[me, 3, rows, columns], 1.0
            ) * jnp.where(inside(near_rank), near[0, 3, rows, columns], 1.0)
        copy_between(chunk).start()

    def merge_pair(chunk):
        copy_near(1, chunk).wait_recv()
        copy_between(chunk).wait_recv()
        rows = rows_of(chunk)
        for columns in tiles:
            own = [pieces[across, k, rows, columns] for k in range(4)]
            other = [near[1, k, rows, columns] for k in range(4)]
            first = jnp.where(own_first, own[3], other[3])
            front = first * between[rows, columns]
            for k in range(3):
                pair_out[k, rows, columns] = jnp.where(
                    own_first, own[k] + front * other[k], other[k] + front * own[k]
                )
            pair_out[3, rows, columns] = first
            pair_out[4, rows, columns] = own[3] * other[3]
        for piece in range(per_chunk):
            copy_pair(chunk * per_chunk + piece).start()

    for owner, chunk in order[2:]:
        load(owner, chunk).start()
    march(across, 0)
    pl.semaphore_wait(barrier, 3 + len(outer_partners))
    copy_raw(0).start()
    march(diagonal, 0)
    copy_raw(1).start()

    @pl.loop(0, chunks + 1)
    def _(chunk):
        @pl.when(chunk < chunks)
        def _():
            march(sibling, chunk)
            copy_near(0, chunk).start()
            march(me, chunk)

        @pl.when(chunk >= 2)
        def _():
            open_between(chunk - 1)

    @pl.loop(1, chunks + 1)
    def _(chunk):
        @pl.when(chunk < chunks)
        def _():
            march(diagonal, chunk)
            copy_near(1, chunk).start()
            march(across, chunk)

        @pl.when(chunk >= 2)
        def _():
            merge_pair(chunk - 1)

    def merge_raw():
        copy_near(0, 0).wait_recv()
        copy_raw(0).wait_recv()
        copy_raw(1).wait_recv()
        rows = rows_of(0)
        across_first = rank_of(across) < rank_of(diagonal)
        for columns in tiles:
            one = [raw[0, k, :, columns] for k in range(4)]
            other = [raw[1, k, :, columns] for k in range(4)]
            first = jnp.where(across_first, one[3], other[3])
            front = first * jnp.where(
                inside(mine_rank), pieces[me, 3, rows, columns], 1.0
            ) * jnp.where(inside(near_rank), near[0, 3, rows, columns], 1.0)
            for k in range(3):
                pair[k, rows, columns] = jnp.where(
                    across_first, one[k] + front * other[k], other[k] + front * one[k]
                )
            pair[3, rows, columns] = first
            pair[4, rows, columns] = one[3] * other[3]

    def composite(piece):
        rows = piece_rows(piece)
        for columns in tiles:
            own = [pieces[me, k, rows, columns] for k in range(4)]
            other = [near[0, k, rows, columns] for k in range(4)]
            far = [pair[k, rows, columns] for k in range(5)]

            def behind_far(value):
                return jnp.where(far_high < value, far[4], jnp.where(far_low < value, far[3], 1.0))

            own_front = behind_far(mine_rank) * jnp.where(own_first, 1.0, other[3])
            other_front = behind_far(near_rank) * jnp.where(own_first, own[3], 1.0)
            far_front = jnp.where(mine_rank < far_low, own[3], 1.0) * jnp.where(
                near_rank < far_low, other[3], 1.0
            )
            for k in range(3):
                banded[k, rows, columns] = (
                    own_front * own[k] + other_front * other[k] + far_front * far[k]
                )
            banded[3, rows, columns] = own[3] * other[3] * far[4]
        for partner in outer_partners:
            copy_outer(partner, group, piece).start()

    ordered = outer_partners + [group]
    group_ranks = [rank[g] for g in ordered]
    mine = pl.ds(pl.multiple_of(group * part, 128), part)

    def finish(piece):
        for partner in outer_partners:
            copy_outer(group, partner, piece).wait_recv()
        rows = piece_rows(piece)

        def value(g, k):
            if g is group:
                return banded[k, rows, mine]
            return groups[g, k, rows, :]

        clear = [value(g, 3) for g in ordered]
        total = [0.0, 0.0, 0.0]
        for i, g in enumerate(ordered):
            front = 1.0
            for j in range(len(ordered)):
                if j != i:
                    front = front * jnp.where(group_ranks[j] < group_ranks[i], clear[j], 1.0)
            total = [total[k] + front * value(g, k) for k in range(3)]
        for k in range(3):
            out[k, rows, :] = total[k]
        through = clear[0]
        for other in clear[1:]:
            through = through * other
        out[3, rows, :] = 1.0 - through
        for partner in outer_partners:
            copy_outer(partner, group, piece).wait_send()

    copy_raw(0).wait_send()
    copy_raw(1).wait_send()
    copy_near(0, 0).wait_send()

    @pl.loop(1, chunks)
    def _(chunk):
        copy_near(0, chunk).wait_send()
        copy_near(1, chunk).wait_send()
        copy_between(chunk).wait_send()

    merge_raw()

    @pl.loop(0, per_chunk)
    def _(piece):
        composite(piece)

    @pl.loop(per_chunk, chunks * per_chunk)
    def _(piece):
        copy_pair(piece).wait_recv()
        composite(piece)
        copy_pair(piece).wait_send()
        finish(piece - LAG)

    @pl.loop(chunks * per_chunk - LAG, chunks * per_chunk)
    def _(piece):
        finish(piece)


def fused(density, extinction, occupancy, colour_slope, slab_rank):
    inner_count = lax.axis_size("inner")
    outer_count = lax.axis_size("outer")
    slices, height, width = density.shape
    band, part = height // inner_count, width // outer_count
    chunks = band // ROWS
    vmem = pl.BlockSpec(memory_space=pltpu.VMEM)
    return pl.pallas_call(
        functools.partial(fused_kernel, inner_count, outer_count),
        out_shape=jax.ShapeDtypeStruct((4, band, part), jnp.float32),
        in_specs=[pl.BlockSpec(memory_space=pl.ANY)] * 5,
        out_specs=vmem,
        scratch_shapes=[
            pltpu.SMEM(extinction.shape, extinction.dtype),
            pltpu.VMEM(occupancy.shape, occupancy.dtype),
            pltpu.SMEM(colour_slope.shape, colour_slope.dtype),
            pltpu.SMEM(slab_rank.shape, slab_rank.dtype),
            pltpu.VMEM((slices, height, width), density.dtype),
            pltpu.VMEM((occupancy.shape[1], width), jnp.float32),
            pltpu.VMEM((inner_count, 4, band, width), jnp.float32),
            pltpu.VMEM((2, 4, ROWS, width), jnp.float32),
            pltpu.VMEM((2, 4, band, width), jnp.float32),
            pltpu.VMEM((band, width), jnp.float32),
            pltpu.VMEM((band, width), jnp.float32),
            pltpu.VMEM((5, band, width), jnp.float32),
            pltpu.VMEM((5, band, width), jnp.float32),
            pltpu.VMEM((4, band, width), jnp.float32),
            pltpu.VMEM((outer_count, 4, band, part), jnp.float32),
            pltpu.SemaphoreType.DMA((4,)),
            pltpu.SemaphoreType.DMA((inner_count, chunks)),
            pltpu.SemaphoreType.DMA((2,)),
            pltpu.SemaphoreType.DMA((2,)),
            pltpu.SemaphoreType.DMA((2, chunks)),
            pltpu.SemaphoreType.DMA((2, chunks)),
            pltpu.SemaphoreType.DMA((chunks,)),
            pltpu.SemaphoreType.DMA((chunks,)),
            pltpu.SemaphoreType.DMA((chunks * ROWS // PIECE,)),
            pltpu.SemaphoreType.DMA((chunks * ROWS // PIECE,)),
            pltpu.SemaphoreType.DMA((outer_count, chunks * ROWS // PIECE)),
            pltpu.SemaphoreType.DMA((outer_count, chunks * ROWS // PIECE)),
        ],
        compiler_params=pltpu.CompilerParams(
            collective_id=0, has_side_effects=True, vmem_limit_bytes=60 * 2**20
        ),
    )(density, extinction, occupancy, colour_slope, slab_rank)


def solution(mesh):
    placed = (
        P(("inner", "outer"), None, "tile"),
        P(("inner", "outer")),
        P(("inner", "outer"), None, "tile"),
        P(),
        P(),
    )

    def local(density, *rest):
        part = density.shape[2] // mesh.shape["outer"]
        band = density.shape[1] // mesh.shape["inner"]
        whole = part % 128 == 0 and band % ROWS == 0 and mesh.shape["inner"] == 4
        return (fused if whole else shards)(density, *rest)

    return jax.shard_map(
        local,
        mesh=mesh,
        in_specs=placed,
        out_specs=P(None, "inner", ("tile", "outer")),
        check_vma=False,
    )
```
